32 devices in a mesh: parts: 2 (over x), loop: 2 (over core), width: 8 (over z, y).
Axes of the slice: x: 2, y: 2, z: 4, core: 2. Of those that a mesh axis runs over, the one named last changes fastest.
Arguments:
- queries: float32 [2048, 65536], P(('parts', 'loop'), 'width'), parts along dimension 0, may hold values from -6 to 6
- store: float32 [4096, 65536], P(('parts', 'loop'), 'width'), parts along dimension 0, may hold values from -0.03125 to 0.03125
Outputs:
- scores: float32 [4096, 1024], P(('parts', 'loop', 'width')), parts along dimension 0
The draws below stay inside these ranges and needn't reach their ends.
There are 2 independent parts, one for each index of `parts`. The reference program is written for one: setup_inputs(seed, part) draws one part's arguments, and reference() takes and returns one part's arrays. A program takes and returns all parts, laid end to end along the dimension named above; each array names one. Nothing has to cross between parts.
All inputs are finite; a program needn't handle non-finite values.
Results may differ from the reference program's by a relative error of at most 0.000071.
Values sent between devices are 32-bit elements; how exact they have to be, the bound alone decides.
A program may use at most 192 MiB of HBM per device.

```python
import jax
import jax.numpy as jnp
from jax import lax

W = 65536
NQ = 1024
STORE_ROWS = 2048


def with_spikes(entries, key, source, target, blocks, factor):
    owner, partner = [(jnp.arange(entries.shape[position]) // (entries.shape[position] // blocks)).reshape([-1 if axis == position else 1 for axis in range(entries.ndim)]) for position in (source, target)]
    chosen = jax.random.permutation(key, blocks)[partner]
    strong = (owner == chosen) | (owner == (partner + blocks // 2) % blocks)
    return jnp.where(strong, factor * entries, entries)


def level_of(stream_key, extent, split, low, high):
    gain, own = 1.0, jax.random.fold_in(stream_key, 6)
    for dim, blocks in split:
        draws = jnp.exp(jax.random.uniform(jax.random.fold_in(own, dim), (blocks,), jnp.float32, low / len(split), high / len(split)))
        gain = gain * jnp.repeat(draws, extent[dim] // blocks).reshape([-1 if axis == dim else 1 for axis in range(len(extent))])
    return gain


def bell_draw(own_key, shape, scale, reach, cuts=(), dtype=jnp.bfloat16):
    array = jax.random.normal(own_key, shape, jnp.float32) * scale
    if len(cuts) > 0:
        array = level_of(own_key, shape, cuts, -0.22, 0.18) * array
    return jnp.clip(array, min=-reach, max=reach).astype(dtype)


def noise_with(key, dims, scale, limit, pieces, heavy, dtype=jnp.bfloat16):
    drawn = scale * jax.random.normal(key, dims, jnp.float32)
    if pieces:
        drawn = drawn * level_of(key, dims, pieces, -0.22, 0.18)
    return jnp.clip(with_spikes(drawn, jax.random.fold_in(key, 3), *heavy), -limit, limit).astype(dtype)


def setup_inputs(seed: int = 0, part: int = 0) -> dict:
    streams_of = jax.random.split(jax.random.key(seed), 3)
    own_keys = jax.random.split(jax.random.fold_in(streams_of[2], part), 3)
    return {
        "queries": bell_draw(own_keys[0], (NQ, W), 1.0, 6.0, ((0, 2), (1, 8)), jnp.float32),
        "store": noise_with(own_keys[1], (STORE_ROWS, W), W ** -0.5, 0.03125, ((0, 2), (1, 8)), (1, 0, 8, 2.0), jnp.float32),
    }


def reference(queries, store):
    inner = jnp.dot(store, queries.T, precision=lax.Precision.HIGHEST, preferred_element_type=jnp.float32)
    return inner
```

```python
import jax
import jax.numpy as jnp
from jax import lax
from jax.sharding import PartitionSpec as P


def shifted(value, axis, steps):
    count = lax.axis_size(axis)
    pairs = [(source, (source + steps) % count) for source in range(count)]
    return lax.ppermute(value, axis, pairs)


def partial_scores(store, panel):
    return lax.dot_general(
        store,
        panel,
        (((1,), (1,)), ((), ())),
        precision=lax.Precision.HIGH,
        preferred_element_type=jnp.float32,
    )


def body(queries, store):
    panel_rows = queries.shape[0]
    loop_size = lax.axis_size("loop")
    here = lax.axis_index("loop")
    panel = queries
    rows = store.shape[0] // lax.axis_size("width")
    out = jnp.zeros((rows, panel_rows * loop_size), jnp.float32)
    for step in range(loop_size):
        owner = (here - step) % loop_size
        part = partial_scores(store, panel)
        if step + 1 < loop_size:
            panel = shifted(panel, "loop", 1)
        part = lax.psum_scatter(part, "width", scatter_dimension=0, tiled=True)
        out = lax.dynamic_update_slice_in_dim(out, part, owner * panel_rows, 1)
    return out


def solution(mesh):
    in_specs = (P(("parts", "loop"), "width"), P(("parts", "loop"), "width"))
    out_specs = P(("parts", "loop", "width"), None)
    return jax.shard_map(body, mesh=mesh, in_specs=in_specs, out_specs=out_specs, check_vma=False)
```

```python
import functools

import jax
import jax.numpy as jnp
from jax import lax
from jax.experimental import pallas as pl
from jax.experimental.pallas import tpu as pltpu
from jax.sharding import PartitionSpec as P

MESH = pl.DeviceIdType.MESH
PIECES = 4


def split(value):
    high = value.astype(jnp.bfloat16)
    low = (value - high.astype(jnp.float32)).astype(jnp.bfloat16)
    return high, low


def dot_t(left, right):
    return lax.dot_general(
        left, right, (((1,), (1,)), ((), ())), preferred_element_type=jnp.float32
    )


def kernel(width, group_rows, cols, depth, q_ref, s_ref, out_ref, rq_ref,
           s_hi, s_lo, q_hi, q_lo, s_stage, q_stage, res, rx1, rx2,
           s_sem, q_sem, xs_sem, xr_sem, as_sem, ar_sem, bs_sem, br_sem):
    here = lax.axis_index("loop")
    me = lax.axis_index("width")
    line, side = me // 2, me % 2
    pairs = width // 2
    store_rows, extent = s_ref.shape
    own = store_rows // width
    groups = store_rows // group_rows
    per_group = pairs // groups
    steps = extent // depth
    panel_rows = q_ref.shape[0]
    own_chunks = panel_rows // cols
    chunks = 2 * own_chunks
    piece = cols // PIECES
    order = []
    for i in range((pairs + 1) // 2):
        order += [i] if i == pairs - 1 - i else [i, pairs - 1 - i]

    barrier = pltpu.get_barrier_semaphore()
    pl.semaphore_signal(barrier, inc=1, device_id={"loop": 1 - here}, device_id_type=MESH)
    pl.semaphore_signal(barrier, inc=1, device_id={"width": line * 2 + 1 - side}, device_id_type=MESH)
    for other in range(1, pairs):
        target = lax.rem(line + other, pairs) * 2 + side
        pl.semaphore_signal(barrier, inc=1, device_id={"width": target}, device_id_type=MESH)

    def s_copies(g, kb, slot):
        return [
            pltpu.make_async_copy(
                s_ref.at[pl.ds(order[g * per_group + k] * 2 * own, 2 * own), pl.ds(pl.multiple_of(kb * depth, depth), depth)],
                s_stage.at[slot, pl.ds(k * 2 * own, 2 * own)],
                s_sem.at[slot, k],
            )
            for k in range(per_group)
        ]

    def q_copy(c, kb, slot):
        source, first = (q_ref, c) if c < own_chunks else (rq_ref, c - own_chunks)
        return pltpu.make_async_copy(
            source.at[pl.ds(first * cols, cols), pl.ds(pl.multiple_of(kb * depth, depth), depth)],
            q_stage.at[slot],
            q_sem.at[slot],
        )

    def exchange(c, m):
        rows = pl.ds(c * cols + m * piece, piece)
        return pltpu.make_async_remote_copy(
            src_ref=q_ref.at[rows], dst_ref=rq_ref.at[rows],
            send_sem=xs_sem.at[c, m], recv_sem=xr_sem.at[c, m],
            device_id={"loop": 1 - here}, device_id_type=MESH,
        )

    def stage_a(u):
        return pltpu.make_async_remote_copy(
            src_ref=res.at[u, :, 1 - side], dst_ref=rx1.at[u],
            send_sem=as_sem.at[u], recv_sem=ar_sem.at[u],
            device_id={"width": line * 2 + 1 - side}, device_id_type=MESH,
        )

    def stage_b(u, k):
        c, g = u // groups, u % groups
        p = order[g * per_group + k]
        return pltpu.make_async_remote_copy(
            src_ref=res.at[u, k, side], dst_ref=rx2.at[line, c],
            send_sem=bs_sem.at[u, k], recv_sem=br_sem.at[line, c],
            device_id={"width": p * 2 + side}, device_id_type=MESH,
        )

    def receive_b(c, source):
        return pltpu.make_async_remote_copy(
            src_ref=rx2.at[source, c], dst_ref=rx2.at[source, c],
            send_sem=bs_sem.at[0, 0], recv_sem=br_sem.at[source, c],
            device_id={"width": source * 2 + side}, device_id_type=MESH,
        )

    def pass_on(u):
        c, g = u // groups, u % groups
        stage_a(u).wait_recv()
        for k in range(per_group):
            res[u, k, side] = res[u, k, side] + rx1[u, k]
            p = order[g * per_group + k]

            @pl.when(p != line)
            def _():
                stage_b(u, k).start()

            @pl.when(p == line)
            def _():
                rx2[line, c] = res[u, k, side]

    def finish(c):
        for source in range(pairs):
            @pl.when(source != line)
            def _():
                receive_b(c, source).wait_recv()
        total = rx2[0, c]
        for source in range(1, pairs):
            total = total + rx2[source, c]
        owner = here if c < own_chunks else 1 - here
        start = pl.multiple_of(owner * panel_rows + (c % own_chunks) * cols, cols)
        out_ref[:, pl.ds(start, cols)] = total

    for copy in s_copies(0, 0, 0):
        copy.start()
    q_copy(0, 0, 0).start()
    pl.semaphore_wait(barrier, pairs + 1)
    for c in range(own_chunks):
        for m in range(PIECES):
            exchange(c, m).start()

    units = chunks * groups
    for u in range(units):
        c, g = u // groups, u % groups
        refill = g == groups - 1 and c + 1 < chunks
        res[u] = jnp.zeros(res.shape[1:], jnp.float32)
        if refill:
            if c + 1 >= own_chunks:
                for m in range(PIECES):
                    exchange(c + 1 - own_chunks, m).wait_recv()
            q_copy(c + 1, 0, 0).start()

        @pl.loop(0, steps)
        def _(kb):
            slot = lax.rem(kb, 2)
            if c == 0:
                @pl.when(kb + 1 < steps)
                def _():
                    for copy in s_copies(g, kb + 1, 1 - slot):
                        copy.start()
            if u == 0 or refill:
                @pl.when(kb + 1 < steps)
                def _():
                    q_copy(0 if u == 0 else c + 1, kb + 1, 1 - slot).start()
            if c == 0:
                for copy in s_copies(g, kb, slot):
                    copy.wait()
                s_hi[g, kb], s_lo[g, kb] = split(s_stage[slot])
            if u == 0:
                q_copy(0, kb, slot).wait()
                q_hi[kb], q_lo[kb] = split(q_stage[slot])
            high = s_hi[g, kb]
            part = dot_t(high, q_hi[kb]) + dot_t(s_lo[g, kb], q_hi[kb]) + dot_t(high, q_lo[kb])
            res[u] += part.reshape(res.shape[1:])
            if refill:
                q_copy(c + 1, kb, slot).wait()
                q_hi[kb], q_lo[kb] = split(q_stage[slot])

        stage_a(u).start()
        if c == 0 and g + 1 < groups:
            for copy in s_copies(g + 1, 0, 0):
                copy.start()
        if u >= 1:
            pass_on(u - 1)
    for c in range(chunks - 1):
        finish(c)
    pass_on(units - 1)
    finish(chunks - 1)
    for u in range(units):
        stage_a(u).wait_send()
        for k in range(per_group):
            @pl.when(order[u % groups * per_group + k] != line)
            def _():
                stage_b(u, k).wait_send()
    for c in range(own_chunks):
        for m in range(PIECES):
            exchange(c, m).wait_send()


def body(width, queries, store):
    panel_rows, extent = queries.shape
    store_rows = store.shape[0]
    own = store_rows // width
    group_rows, cols, depth = 512, 256, 1024
    groups, steps = store_rows // group_rows, extent // depth
    chunks = 2 * panel_rows // cols
    pairs = width // 2
    per_group = pairs // groups
    units = chunks * groups
    f32, bf16 = jnp.float32, jnp.bfloat16
    dma = pltpu.SemaphoreType.DMA
    out, _ = pl.pallas_call(
        functools.partial(kernel, width, group_rows, cols, depth),
        out_shape=(
            jax.ShapeDtypeStruct((own, 2 * panel_rows), f32),
            jax.ShapeDtypeStruct((panel_rows, extent), f32),
        ),
        in_specs=[pl.BlockSpec(memory_space=pl.ANY)] * 2,
        out_specs=(pl.BlockSpec(memory_space=pltpu.VMEM), pl.BlockSpec(memory_space=pl.ANY)),
        scratch_shapes=[
            pltpu.VMEM((groups, steps, group_rows, depth), bf16),
            pltpu.VMEM((groups, steps, group_rows, depth), bf16),
            pltpu.VMEM((steps, cols, depth), bf16),
            pltpu.VMEM((steps, cols, depth), bf16),
            pltpu.VMEM((2, group_rows, depth), f32),
            pltpu.VMEM((2, cols, depth), f32),
            pltpu.VMEM((units, per_group, 2, own, cols), f32),
            pltpu.VMEM((units, per_group, own, cols), f32),
            pltpu.VMEM((pairs, chunks, own, cols), f32),
            dma((2, per_group)),
            dma((2,)),
            dma((chunks // 2, PIECES)),
            dma((chunks // 2, PIECES)),
            dma((units,)),
            dma((units,)),
            dma((units, per_group)),
            dma((pairs, chunks)),
        ],
        compiler_params=pltpu.CompilerParams(
            collective_id=0, has_side_effects=True, vmem_limit_bytes=62 * 2**20
        ),
        cost_estimate=pl.CostEstimate(
            flops=12 * store_rows * panel_rows * extent,
            bytes_accessed=4 * extent * (store_rows + 3 * panel_rows),
            transcendentals=0,
        ),
    )(queries, store)
    return out


def solution(mesh):
    in_specs = (P(("parts", "loop"), "width"), P(("parts", "loop"), "width"))
    out_specs = P(("parts", "loop", "width"), None)
    step = functools.partial(body, mesh.shape["width"])
    return jax.shard_map(step, mesh=mesh, in_specs=in_specs, out_specs=out_specs, check_vma=False)
```

```python
import functools

import jax
import jax.numpy as jnp
from jax import lax
from jax.experimental import pallas as pl
from jax.experimental.pallas import tpu as pltpu
from jax.sharding import PartitionSpec as P

MESH = pl.DeviceIdType.MESH
PIECES = 4


def split(value):
    high = value.astype(jnp.bfloat16)
    low = (value - high.astype(jnp.float32)).astype(jnp.bfloat16)
    return high, low


def dot_t(left, right):
    return lax.dot_general(
        left, right, (((1,), (1,)), ((), ())), preferred_element_type=jnp.float32
    )


def kernel(width, group_rows, cols, depth, q_ref, s_ref, out_ref, rq_ref,
           s_hi, s_lo, q_hi, q_lo, s_stage, q_stage, res, rx1, rx2,
           s_sem, q_sem, xs_sem, xr_sem, as_sem, ar_sem, bs_sem, br_sem):
    here = lax.axis_index("loop")
    me = lax.axis_index("width")
    line, side = me // 2, me % 2
    pairs = width // 2
    store_rows, extent = s_ref.shape
    own = store_rows // width
    groups = store_rows // group_rows
    per_group = pairs // groups
    steps = extent // depth
    panel_rows = q_ref.shape[0]
    own_chunks = panel_rows // cols
    chunks = 2 * own_chunks
    piece = cols // PIECES
    order = []
    for i in range((pairs + 1) // 2):
        order += [i] if i == pairs - 1 - i else [i, pairs - 1 - i]

    barrier = pltpu.get_barrier_semaphore()
    pl.semaphore_signal(barrier, inc=1, device_id={"loop": 1 - here}, device_id_type=MESH)
    pl.semaphore_signal(barrier, inc=1, device_id={"width": line * 2 + 1 - side}, device_id_type=MESH)
    for other in range(1, pairs):
        target = lax.rem(line + other, pairs) * 2 + side
        pl.semaphore_signal(barrier, inc=1, device_id={"width": target}, device_id_type=MESH)

    def s_copies(g, kb, slot):
        return [
            pltpu.make_async_copy(
                s_ref.at[pl.ds(order[g * per_group + k] * 2 * own, 2 * own), pl.ds(pl.multiple_of(kb * depth, depth), depth)],
                s_stage.at[slot, pl.ds(k * 2 * own, 2 * own)],
                s_sem.at[slot, k],
            )
            for k in range(per_group)
        ]

    def q_copy(c, kb, slot):
        source, first = (q_ref, c) if c < own_chunks else (rq_ref, c - own_chunks)
        return pltpu.make_async_copy(
            source.at[pl.ds(first * cols, cols), pl.ds(pl.multiple_of(kb * depth, depth), depth)],
            q_stage.at[slot],
            q_sem.at[slot],
        )

    def exchange(c, m):
        rows = pl.ds(c * cols + m * piece, piece)
        return pltpu.make_async_remote_copy(
            src_ref=q_ref.at[rows], dst_ref=rq_ref.at[rows],
            send_sem=xs_sem.at[c, m], recv_sem=xr_sem.at[c, m],
            device_id={"loop": 1 - here}, device_id_type=MESH,
        )

    def stage_a(u):
        return pltpu.make_async_remote_copy(
            src_ref=res.at[u, :, 1 - side], dst_ref=rx1.at[u],
            send_sem=as_sem.at[u], recv_sem=ar_sem.at[u],
            device_id={"width": line * 2 + 1 - side}, device_id_type=MESH,
        )

    def stage_b(u, k):
        c, g = u // groups, u % groups
        p = order[g * per_group + k]
        return pltpu.make_async_remote_copy(
            src_ref=res.at[u, k, side], dst_ref=rx2.at[line, c],
            send_sem=bs_sem.at[u, k], recv_sem=br_sem.at[line, c],
            device_id={"width": p * 2 + side}, device_id_type=MESH,
        )

    def receive_b(c, source):
        return pltpu.make_async_remote_copy(
            src_ref=rx2.at[source, c], dst_ref=rx2.at[source, c],
            send_sem=bs_sem.at[0, 0], recv_sem=br_sem.at[source, c],
            device_id={"width": source * 2 + side}, device_id_type=MESH,
        )

    def pass_on(u):
        c, g = u // groups, u % groups
        stage_a(u).wait_recv()
        for k in range(per_group):
            res[u, k, side] = res[u, k, side] + rx1[u, k]
            p = order[g * per_group + k]

            @pl.when(p != line)
            def _():
                stage_b(u, k).start()

            @pl.when(p == line)
            def _():
                rx2[line, c] = res[u, k, side]

    def finish(c):
        for source in range(pairs):
            @pl.when(source != line)
            def _():
                receive_b(c, source).wait_recv()
        total = rx2[0, c]
        for source in range(1, pairs):
            total = total + rx2[source, c]
        owner = here if c < own_chunks else 1 - here
        start = pl.multiple_of(owner * panel_rows + (c % own_chunks) * cols, cols)
        out_ref[:, pl.ds(start, cols)] = total

    for copy in s_copies(0, 0, 0):
        copy.start()
    q_copy(0, 0, 0).start()
    pl.semaphore_wait(barrier, pairs + 1)
    for c in range(own_chunks):
        for m in range(PIECES):
            exchange(c, m).start()

    units = chunks * groups
    for u in range(units):
        c, g = u // groups, u % groups
        refill = g == groups - 1 and c + 1 < chunks
        res[u] = jnp.zeros(res.shape[1:], jnp.float32)
        if refill:
            if c + 1 >= own_chunks:
                for m in range(PIECES):
                    exchange(c + 1 - own_chunks, m).wait_recv()
            q_copy(c + 1, 0, 0).start()

        @pl.loop(0, steps)
        def _(kb):
            slot = lax.rem(kb, 2)
            if c == 0:
                @pl.when(kb + 1 < steps)
                def _():
                    for copy in s_copies(g, kb + 1, 1 - slot):
                        copy.start()
            if u == 0 or refill:
                @pl.when(kb + 1 < steps)
                def _():
                    q_copy(0 if u == 0 else c + 1, kb + 1, 1 - slot).start()
            if c == 0:
                for copy in s_copies(g, kb, slot):
                    copy.wait()
                s_hi[g, kb], s_lo[g, kb] = split(s_stage[slot])
            if u == 0:
                q_copy(0, kb, slot).wait()
                q_hi[kb], q_lo[kb] = split(q_stage[slot])
            high = s_hi[g, kb]
            part = dot_t(
                jnp.concatenate([high, s_lo[g, kb], high], 1),
                jnp.concatenate([q_hi[kb], q_hi[kb], q_lo[kb]], 1),
            )
            res[u] += part.reshape(res.shape[1:])
            if refill:
                q_copy(c + 1, kb, slot).wait()
                q_hi[kb], q_lo[kb] = split(q_stage[slot])

        stage_a(u).start()
        if c == 0 and g + 1 < groups:
            for copy in s_copies(g + 1, 0, 0):
                copy.start()
        if u >= 1:
            pass_on(u - 1)
    for c in range(chunks - 1):
        finish(c)
    pass_on(units - 1)
    finish(chunks - 1)
    for u in range(units):
        stage_a(u).wait_send()
        for k in range(per_group):
            @pl.when(order[u % groups * per_group + k] != line)
            def _():
                stage_b(u, k).wait_send()
    for c in range(own_chunks):
        for m in range(PIECES):
            exchange(c, m).wait_send()


def body(width, queries, store):
    panel_rows, extent = queries.shape
    store_rows = store.shape[0]
    own = store_rows // width
    group_rows, cols, depth = 512, 256, 1024
    groups, steps = store_rows // group_rows, extent // depth
    chunks = 2 * panel_rows // cols
    pairs = width // 2
    per_group = pairs // groups
    units = chunks * groups
    f32, bf16 = jnp.float32, jnp.bfloat16
    dma = pltpu.SemaphoreType.DMA
    out, _ = pl.pallas_call(
        functools.partial(kernel, width, group_rows, cols, depth),
        out_shape=(
            jax.ShapeDtypeStruct((own, 2 * panel_rows), f32),
            jax.ShapeDtypeStruct((panel_rows, extent), f32),
        ),
        in_specs=[pl.BlockSpec(memory_space=pl.ANY)] * 2,
        out_specs=(pl.BlockSpec(memory_space=pltpu.VMEM), pl.BlockSpec(memory_space=pl.ANY)),
        scratch_shapes=[
            pltpu.VMEM((groups, steps, group_rows, depth), bf16),
            pltpu.VMEM((groups, steps, group_rows, depth), bf16),
            pltpu.VMEM((steps, cols, depth), bf16),
            pltpu.VMEM((steps, cols, depth), bf16),
            pltpu.VMEM((2, group_rows, depth), f32),
            pltpu.VMEM((2, cols, depth), f32),
            pltpu.VMEM((units, per_group, 2, own, cols), f32),
            pltpu.VMEM((units, per_group, own, cols), f32),
            pltpu.VMEM((pairs, chunks, own, cols), f32),
            dma((2, per_group)),
            dma((2,)),
            dma((chunks // 2, PIECES)),
            dma((chunks // 2, PIECES)),
            dma((units,)),
            dma((units,)),
            dma((units, per_group)),
            dma((pairs, chunks)),
        ],
        compiler_params=pltpu.CompilerParams(
            collective_id=0, has_side_effects=True, vmem_limit_bytes=62 * 2**20
        ),
        cost_estimate=pl.CostEstimate(
            flops=12 * store_rows * panel_rows * extent,
            bytes_accessed=4 * extent * (store_rows + 3 * panel_rows),
            transcendentals=0,
        ),
    )(queries, store)
    return out


def solution(mesh):
    in_specs = (P(("parts", "loop"), "width"), P(("parts", "loop"), "width"))
    out_specs = P(("parts", "loop", "width"), None)
    step = functools.partial(body, mesh.shape["width"])
    return jax.shard_map(step, mesh=mesh, in_specs=in_specs, out_specs=out_specs, check_vma=False)
```
